768 devices in a mesh: dap: 24 (over x_lo, z), ctx: 32 (over y, x_hi, core).
Axes of the slice: x: 4 (x_hi: 2, x_lo: 2; x = x_hi * 2 + x_lo), y: 8, z: 12, core: 2. Of those that a mesh axis runs over, the one named last changes fastest.
Arguments:
- pair: bfloat16 [2304, 48, 128], P(('ctx', 'dap')), may hold values from -6 to 6
- cotangent: bfloat16 [2304, 48, 128], P(('ctx', 'dap')), may hold values from -6 to 6
- residue_mask: int32 [2304], replicated, may hold values 0 or 1
- bias: float32 [4, 2304, 2304], P(None, 'ctx'), may hold values from -250 to 250
- ln_attend: float32 [128], replicated, may hold values from 0.1 to 1.9
- w_in: bfloat16 [128, 512], replicated, may hold values from -0.5 to 0.5
- w_out: bfloat16 [128, 128], replicated, may hold values from -0.5 to 0.5
- ln_trans: float32 [128], replicated, may hold values from 0.1 to 1.9
- w_up: bfloat16 [128, 512], replicated, may hold values from -0.5 to 0.5
- w_down: bfloat16 [512, 128], replicated, may hold values from -0.25 to 0.25
Outputs:
- pair_grad: float32 [2304, 48, 128], P(('ctx', 'dap'))
- bias_grad: float32 [4, 2304, 2304], P(None, 'ctx', 'dap')
The draws below stay inside these ranges and needn't reach their ends.
All inputs are finite; a program needn't handle non-finite values.
Results may differ from the reference program's by a relative error of at most 0.01.
Values may be sent and summed in bfloat16 or wider, within the bound.
No kernel may reach another device: no remote copies, remote signals or barrier semaphores. Data moves between devices by JAX's collectives and lax.ppermute only.
A program may use at most 64 MiB of HBM per device.

```python
from functools import partial
import jax
import jax.numpy as jnp
from jax import lax

C = 128
H = 4
DH = 32
FT = 512
N = 2304
J = 48


def draw_bias(key, part):
    key = jax.random.fold_in(key, 7)
    base_key = jax.random.fold_in(key, 0)
    return 2.0 * jax.random.normal(base_key, (H, N, N), jnp.float32)


def place_ends(entries, own_key, low, high):
    longest = entries.shape.index(max(entries.shape))
    spots = []
    for shift in (0, 1):
        where = [jax.random.randint(jax.random.fold_in(own_key, axis), (), 0, length) for axis, length in enumerate(entries.shape)]
        where[longest] = (where[longest] + shift) % entries.shape[longest]
        spots.append(tuple(where))
    return entries.at[spots[0]].set(low).at[spots[1]].set(high)


def block_levels(stream_key, shape, pieces, low, high):
    factor_of = 1.0
    for position, blocks in pieces:
        steps = jax.random.uniform(jax.random.fold_in(jax.random.fold_in(stream_key, 6), position), (blocks,), jnp.float32, low / len(pieces), high / len(pieces))
        factor_of = factor_of * jnp.repeat(jnp.exp(steps), shape[position] // blocks).reshape((-1,) + (1,) * (len(shape) - 1 - position))
    return factor_of


def scatter_about(rng, shape, width, limit, shards=(), held_as=jnp.bfloat16):
    array = jax.random.normal(rng, shape, jnp.float32) * width
    if len(shards) > 0:
        array = block_levels(rng, shape, shards, -0.22, 0.18) * array
    return jnp.clip(array, min=-limit, max=limit).astype(held_as)


def setup_inputs(seed: int = 0) -> dict:
    arg_keys = jax.random.split(jax.random.key(seed), 11)
    return {
        "pair": scatter_about(arg_keys[0], (N, J, C), 1.0, 6.0, ((0, 768),)),
        "cotangent": scatter_about(arg_keys[1], (N, J, C), 1.0, 6.0, ((0, 768),)),
        "residue_mask": place_ends((jax.random.randint(arg_keys[2], (N,), 0, 4) < 3).astype(jnp.int32), jax.random.fold_in(arg_keys[2], 1), 0, 1),
        "bias": draw_bias(jax.random.fold_in(arg_keys[10], 71), 0),
        "ln_attend": jnp.clip(1.0 + 0.18 * jax.random.normal(arg_keys[4], (C,), jnp.float32), 0.1, 1.9),
        "w_in": scatter_about(arg_keys[5], (C, 4 * H * DH), C ** -0.5, 0.5),
        "w_out": scatter_about(arg_keys[6], (H * DH, C), (H * DH) ** -0.5, 0.5),
        "ln_trans": jnp.clip(1.0 + 0.18 * jax.random.normal(arg_keys[7], (C,), jnp.float32), 0.1, 1.9),
        "w_up": scatter_about(arg_keys[8], (C, FT), C ** -0.5, 0.5),
        "w_down": scatter_about(arg_keys[9], (FT, C), FT ** -0.5, 0.25),
    }


def layer_norm(inputs, gain):
    average = lax.optimization_barrier(jnp.mean(inputs, axis=-1, keepdims=True))
    centred = inputs - average
    variance = lax.optimization_barrier(jnp.mean(centred * centred, axis=-1, keepdims=True))
    return centred * lax.rsqrt(variance + 1e-05) * gain

def flat_dot(inputs, weight):
    leading = inputs.shape[:-1]
    result = jnp.dot(inputs.reshape(-1, inputs.shape[-1]), weight, preferred_element_type=jnp.float32)
    return result.reshape(leading + (weight.shape[1],))

def exact_dot(inputs, weight):
    leading = inputs.shape[:-1]
    result = jnp.dot(inputs.reshape(-1, inputs.shape[-1]), weight, preferred_element_type=jnp.float32, precision=lax.Precision.HIGHEST)
    return result.reshape(leading + (weight.shape[1],))

def mix(pattern, first_op, second_op):
    return jnp.einsum(pattern, first_op.astype(jnp.float32), second_op.astype(jnp.float32))

def split_heads(tensor):
    return tensor.reshape(tensor.shape[0], tensor.shape[1], H, DH)

def merge_heads(tensor):
    return tensor.reshape(tensor.shape[0], tensor.shape[1], H * DH)

def attend_forward(queries, keys_all, values_all, bias_rows, key_bias):
    scale = DH ** (-0.5)
    scores = mix('ijhd,kjhd->hijk', split_heads(queries), split_heads(keys_all)) * scale
    scores = scores + bias_rows[:, :, None, :] + key_bias
    row_max = lax.optimization_barrier(jnp.max(scores, axis=-1, keepdims=True))
    exponent = jnp.exp(scores - row_max)
    weights = exponent / lax.optimization_barrier(jnp.sum(exponent, axis=-1, keepdims=True))
    weights_b = weights.astype(jnp.bfloat16)
    heads_out = merge_heads(mix('hijk,kjhd->ijhd', weights_b, split_heads(values_all)))
    return (weights, weights_b, heads_out)

def attend_backward(queries, keys_all, values_all, weights, weights_b, d_heads):
    scale = DH ** (-0.5)
    d_heads_b = split_heads(d_heads.astype(jnp.bfloat16))
    d_weights = mix('ijhd,kjhd->hijk', d_heads_b, split_heads(values_all))
    row_dot = lax.optimization_barrier(jnp.sum(weights * d_weights, axis=-1, keepdims=True))
    d_scores = weights * (d_weights - row_dot)
    d_scores_b = d_scores.astype(jnp.bfloat16)
    d_query = merge_heads(mix('hijk,kjhd->ijhd', d_scores_b, split_heads(keys_all))) * scale
    d_key = merge_heads(mix('hijk,ijhd->kjhd', d_scores_b, split_heads(queries))) * scale
    d_value = merge_heads(mix('hijk,ijhd->kjhd', weights_b, d_heads_b))
    d_bias = lax.optimization_barrier(jnp.sum(d_scores, axis=2))
    return (d_query, d_key, d_value, d_bias)

def transition_back(residual_mid, cotangent_cols, ln_trans, w_up, w_down):
    trans_in, trans_back = jax.vjp(partial(layer_norm, gain=ln_trans), residual_mid)
    pre_act = flat_dot(trans_in.astype(jnp.bfloat16), w_up)
    gate_s = jax.nn.sigmoid(pre_act)
    slope = gate_s + pre_act * gate_s * (1.0 - gate_s)
    d_hidden = (flat_dot(cotangent_cols, w_down.T) * slope).astype(jnp.bfloat16)
    d_trans = flat_dot(d_hidden, w_up.T)
    return cotangent_cols.astype(jnp.float32) + trans_back(d_trans)[0]

def column_grads(column_pair, column_cot, bias, key_bias, ln_attend, w_in, w_out, ln_trans, w_up, w_down):
    inner_width = H * DH
    source = column_pair.astype(jnp.float32)
    normed, norm_back = jax.vjp(partial(layer_norm, gain=ln_attend), source)
    projected = flat_dot(normed.astype(jnp.bfloat16), w_in)
    queries = projected[..., :inner_width].astype(jnp.bfloat16)
    keys_all = projected[..., inner_width:2 * inner_width].astype(jnp.bfloat16)
    values_all = projected[..., 2 * inner_width:3 * inner_width].astype(jnp.bfloat16)
    gate_raw = projected[..., 3 * inner_width:]
    weights, weights_b, heads_out = attend_forward(queries, keys_all, values_all, bias, key_bias)
    gate_open = jax.nn.sigmoid(gate_raw)
    gated = (heads_out * gate_open).astype(jnp.bfloat16)
    residual_mid = source + flat_dot(gated, w_out)
    d_mid = transition_back(residual_mid, column_cot, ln_trans, w_up, w_down)
    d_gated = flat_dot(d_mid.astype(jnp.bfloat16), w_out.T)
    d_heads = d_gated * gate_open
    d_gate = d_gated * heads_out * gate_open * (1.0 - gate_open)
    d_query, d_key, d_value, d_bias = attend_backward(queries, keys_all, values_all, weights, weights_b, d_heads)
    w_full = w_in.astype(jnp.float32)
    d_normed = exact_dot(d_query, w_full[:, :inner_width].T) + exact_dot(d_gate, w_full[:, 3 * inner_width:].T)
    d_normed = d_normed + exact_dot(d_key, w_full[:, inner_width:2 * inner_width].T)
    d_normed = d_normed + exact_dot(d_value, w_full[:, 2 * inner_width:3 * inner_width].T)
    d_pair = d_mid + norm_back(d_normed)[0]
    return (d_pair, d_bias)

def reference(pair, cotangent, residue_mask, bias, ln_attend, w_in, w_out, ln_trans, w_up, w_down):
    live_keys = residue_mask.astype(jnp.float32)
    key_bias = (live_keys - 1.0) * 1000000000.0

    def per_column(running, inputs):
        column_pair, column_cot = inputs
        d_pair, d_bias = column_grads(column_pair[:, None, :], column_cot[:, None, :], bias, key_bias, ln_attend, w_in, w_out, ln_trans, w_up, w_down)
        return (running + d_bias, d_pair[:, 0, :])
    initial = jnp.zeros((H, N, N), jnp.float32)
    bias_grad, columns = lax.scan(per_column, initial, (jnp.swapaxes(pair, 0, 1), jnp.swapaxes(cotangent, 0, 1)))
    return (jnp.swapaxes(columns, 0, 1), bias_grad)
```

```python
import numpy as np

import jax
import jax.numpy as jnp
from jax import lax
from jax.experimental import pallas as pl
from jax.experimental.pallas import tpu as pltpu
from jax.sharding import PartitionSpec as P

C = 128
H = 4
DH = 32
SCALE = DH ** (-0.5)
F32 = jnp.float32
BF16 = jnp.bfloat16

CORES = [[2 * m, 2 * m + 1] for m in range(16)]
CHIPS = [[2 * m + r for m in range(16)] for r in range(2)]


def mm(a, b):
    return jnp.dot(a, b, preferred_element_type=F32)


def mm_t(a, b):
    return lax.dot_general(a, b, (((1,), (1,)), ((), ())), preferred_element_type=F32)


def halves(x):
    hi = x.astype(BF16)
    return hi, (x - hi.astype(F32)).astype(BF16)


def center(x):
    mean = jnp.mean(x, axis=-1, keepdims=True)
    cen = x - mean
    var = jnp.mean(cen * cen, axis=-1, keepdims=True)
    rstd = lax.rsqrt(var + 1e-05)
    return cen * rstd, rstd


def center_back(hat, rstd, gain, d_out):
    t = d_out * gain
    a = jnp.mean(t, axis=-1, keepdims=True)
    b = jnp.mean(t * hat, axis=-1, keepdims=True)
    return rstd * (t - a - hat * b)


def prep_kernel(x_ref, order_ref, gain_ref, normed_ref, both_ref):
    both = mm(order_ref[...], x_ref[...])
    both_ref[...] = both
    hat, _ = center(both[: both.shape[0] // 2])
    normed_ref[...] = (hat * gain_ref[...]).astype(BF16)


def main_kernel(
    g_ref, normed_ref, both_ref, bias_ref, mask_ref, w_in_ref, w_out_ref, gain_ref, w_up_ref, w_down_ref,
    db_ref, dn_ref, loc_ref,
    k_scr, v_scr, s_scr, w_scr, wb_scr, ds_scr, dsb_scr, dn_scr,
):
    n = bias_ref.shape[1]
    rows = bias_ref.shape[0] // H
    cols = 2

    def make_kv(p, _):
        parts = []
        for core in range(2):
            start = pl.multiple_of((core * (n // (2 * rows)) + p) * (cols * rows), cols * rows)
            x = g_ref[pl.ds(start, cols * rows), :]
            parts.append(mm(x, w_in_ref[:, C : 3 * C]))
        dest = pl.multiple_of(p * 2 * rows, 2 * rows)
        for j in range(cols):
            kv = jnp.concatenate([q[j * rows : (j + 1) * rows] for q in parts], axis=0).astype(BF16)
            k_scr[j, pl.ds(dest, 2 * rows), :] = kv[:, :C]
            v_scr[j, pl.ds(dest, 2 * rows), :] = kv[:, C:]
        return 0

    lax.fori_loop(0, n // (2 * rows), make_kv, 0)

    normed = normed_ref[...]
    queries = mm(normed, w_in_ref[:, :C])
    gate_raw = mm(normed, w_in_ref[:, 3 * C :])
    key_bias = (mask_ref[...].astype(F32) - 1.0) * 1000000000.0

    def head_mask(h):
        lane = lax.broadcasted_iota(jnp.int32, (rows, C), 1)
        return (lane >= h * DH) & (lane < (h + 1) * DH)

    def stack(x):
        return jnp.concatenate([jnp.where(head_mask(h), x, 0.0) for h in range(H)], axis=0).astype(BF16)

    def unstack(x):
        out = jnp.where(head_mask(0), x[:rows], 0.0)
        for h in range(1, H):
            out = jnp.where(head_mask(h), x[h * rows : (h + 1) * rows], out)
        return out

    q_stack = [stack(queries[j * rows : (j + 1) * rows]) for j in range(cols)]
    heads = []
    for j in range(cols):
        s_scr[...] = mm_t(q_stack[j], k_scr[j])

        def soft(r, _, j=j):
            at = pl.ds(pl.multiple_of(r * 16, 16), 16)
            s = s_scr[at, :] * SCALE + bias_ref[at, :] + key_bias
            e = jnp.exp(s - jnp.max(s, axis=-1, keepdims=True))
            w = e * (1.0 / jnp.sum(e, axis=-1, keepdims=True))
            w_scr[j, at, :] = w
            wb_scr[j, at, :] = w.astype(BF16)
            return 0

        lax.fori_loop(0, H * rows // 16, soft, 0, unroll=2)
        heads.append(unstack(mm(wb_scr[j], v_scr[j])))
    heads_out = jnp.concatenate(heads, axis=0)

    open_ = jax.nn.sigmoid(gate_raw)
    both = both_ref[...]
    source, cot = both[: cols * rows], both[cols * rows :]
    gated = (heads_out * open_).astype(BF16)
    mid = source + mm(gated, w_out_ref[...])
    mid_hat, mid_rstd = center(mid)
    gain = gain_ref[...]
    pre = mm((mid_hat * gain).astype(BF16), w_up_ref[...])
    gs = jax.nn.sigmoid(pre)
    slope = gs + pre * gs * (1.0 - gs)
    d_hidden = (mm_t(cot.astype(BF16), w_down_ref[...]) * slope).astype(BF16)
    d_trans = mm_t(d_hidden, w_up_ref[...])
    d_mid = cot + center_back(mid_hat, mid_rstd, gain, d_trans)
    d_gated = mm_t(d_mid.astype(BF16), w_out_ref[...])
    d_heads = d_gated * open_
    d_gate = d_gated * heads_out * open_ * (1.0 - open_)
    loc_ref[: cols * rows, :] = d_mid

    w_kv = w_in_ref[:, C : 3 * C]
    d_query = []
    for j in range(cols):
        do_stack = stack(d_heads[j * rows : (j + 1) * rows])
        s_scr[...] = mm_t(do_stack, v_scr[j])

        def back(r, _, j=j):
            at = pl.ds(pl.multiple_of(r * 16, 16), 16)
            w = w_scr[j, at, :]
            dw = s_scr[at, :]
            ds = w * (dw - jnp.sum(w * dw, axis=-1, keepdims=True))
            dsb_scr[at, :] = ds.astype(BF16)
            if j == 0:
                ds_scr[at, :] = ds
            else:
                ds_scr[at, :] = ds_scr[at, :] + ds
            return 0

        lax.fori_loop(0, H * rows // 16, back, 0, unroll=2)
        ds_b = dsb_scr[...]
        d_query.append(unstack(mm(ds_b, k_scr[j])) * SCALE)
        dk = mm(q_stack[j].astype(F32).T.astype(BF16), ds_b) * SCALE
        dv = mm(do_stack.astype(F32).T.astype(BF16), wb_scr[j])
        hi, lo = halves(jnp.concatenate([dk, dv], axis=0))
        dn_scr[j] = (mm(w_kv, hi) + mm(w_kv, lo)).T

    hi, lo = halves(jnp.concatenate([jnp.concatenate(d_query, axis=0), d_gate], axis=1))
    w_qg = jnp.concatenate([w_in_ref[:, :C], w_in_ref[:, 3 * C :]], axis=1)
    loc_ref[cols * rows :, :] = mm_t(hi, w_qg) + mm_t(lo, w_qg)

    def put_dn(p, _):
        for core in range(2):
            at = pl.multiple_of((2 * p + core) * rows, rows)
            block = jnp.concatenate([dn_scr[j, pl.ds(at, rows), :] for j in range(cols)], axis=0)
            start = pl.multiple_of((core * (n // (2 * rows)) + p) * (cols * rows), cols * rows)
            dn_ref[pl.ds(start, cols * rows), :] = block.astype(BF16)
        return 0

    lax.fori_loop(0, n // (2 * rows), put_dn, 0)

    def put_db(t, _):
        at = pl.ds(pl.multiple_of(t * C, C), C)
        xs = [ds_scr[pl.ds(h * rows, rows), at] for h in range(H)]
        groups = []
        for a in range(4):
            out = xs[a]
            for h in range(H):
                if h != a:
                    out = jnp.where(head_mask(h), pltpu.roll(xs[h], ((h - a) * DH) % C, 1), out)
            groups.append(out)
        start = pl.multiple_of(t * 4 * rows, 4 * rows)
        db_ref[pl.ds(start, 4 * rows), :] = jnp.concatenate(groups, axis=0).astype(BF16)
        return 0

    lax.fori_loop(0, n // C, put_db, 0)


def last_kernel(parts_ref, loc_ref, both_ref, gain_ref, order_ref, out_ref):
    half = loc_ref.shape[0] // 2
    total = loc_ref[half:, :]
    for p in range(parts_ref.shape[0]):
        total = total + parts_ref[p].astype(F32)
    hat, rstd = center(both_ref[:half, :])
    d_pair = loc_ref[:half, :] + center_back(hat, rstd, gain_ref[...], total)
    out_ref[...] = mm(order_ref[...], d_pair.astype(BF16)).astype(BF16)


def bias_kernel(parts_ref, out_ref):
    rows = out_ref.shape[1]
    total = parts_ref[0].astype(F32)
    for p in range(1, parts_ref.shape[0]):
        total = total + parts_ref[p].astype(F32)
    for h in range(H):
        out_ref[h] = jnp.concatenate(
            [total[t * rows : (t + 1) * rows, h * DH : (h + 1) * DH] for t in range(3)], axis=1
        )


def call(kernel, out_shape, scratch=(), limit=48):
    return pl.pallas_call(
        kernel,
        out_shape=out_shape,
        scratch_shapes=list(scratch),
        compiler_params=pltpu.CompilerParams(vmem_limit_bytes=limit * 1024 * 1024),
    )


def one_hot(source_of):
    out = np.zeros((len(source_of), len(source_of)), np.float32)
    out[np.arange(len(source_of)), source_of] = 1.0
    return out


def per_device(pair, cotangent, residue_mask, bias, ln_attend, w_in, w_out, ln_trans, w_up, w_down):
    n_dap = lax.axis_size("dap")
    n_ctx = lax.axis_size("ctx")
    local, n_cols, _ = pair.shape
    cols = n_cols // n_dap
    rows = local * n_dap
    n = rows * n_ctx
    block = cols * rows
    each = cols * local

    both = jnp.stack([pair, cotangent]).reshape(2, local, n_dap, cols, C)
    both = both.transpose(2, 0, 3, 1, 4).reshape(n_dap * 2 * each, C)
    both = lax.all_to_all(both, "dap", 0, 0, tiled=True)
    source_of = [
        (i // local) * 2 * each + a * each + j * local + i % local
        for a in range(2)
        for j in range(cols)
        for i in range(rows)
    ]
    normed, both = call(
        prep_kernel,
        (jax.ShapeDtypeStruct((block, C), BF16), jax.ShapeDtypeStruct((2 * block, C), F32)),
    )(both, jnp.asarray(one_hot(source_of), BF16), ln_attend[None])

    gathered = normed
    gathered = jnp.broadcast_to(gathered[None], (16, block, C)).reshape(16 * block, C)
    gathered = lax.all_to_all(gathered, "ctx", 0, 0, tiled=True, axis_index_groups=CHIPS)
    other = lax.ppermute(gathered, "ctx", [(i, i ^ 1) for i in range(n_ctx)])
    first = lax.axis_index("ctx") % 2 == 0
    gathered = jnp.concatenate([jnp.where(first, gathered, other), jnp.where(first, other, gathered)], axis=0)

    db, dn, loc = call(
        main_kernel,
        (
            jax.ShapeDtypeStruct((n // DH * rows, C), BF16),
            jax.ShapeDtypeStruct((n * cols, C), BF16),
            jax.ShapeDtypeStruct((2 * block, C), F32),
        ),
        scratch=(
            pltpu.VMEM((cols, n, C), BF16),
            pltpu.VMEM((cols, n, C), BF16),
            pltpu.VMEM((H * rows, n), F32),
            pltpu.VMEM((cols, H * rows, n), F32),
            pltpu.VMEM((cols, H * rows, n), BF16),
            pltpu.VMEM((H * rows, n), F32),
            pltpu.VMEM((H * rows, n), BF16),
            pltpu.VMEM((cols, n, C), F32),
        ),
        limit=56,
    )(
        gathered, normed, both, bias.reshape(H * rows, n), residue_mask[None], w_in, w_out, ln_trans[None],
        w_up, w_down,
    )

    db = lax.all_to_all(db, "dap", 0, 0, tiled=True).reshape(n_dap, n // n_dap // DH * rows, C)
    bias_grad = call(bias_kernel, jax.ShapeDtypeStruct((H, rows, n // n_dap), F32))(db)

    dn = lax.all_to_all(dn, "ctx", 0, 0, tiled=True, axis_index_groups=CORES)
    dn = dn.reshape(2, 16 * block, C).astype(F32).sum(0).astype(BF16)
    dn = lax.all_to_all(dn, "ctx", 0, 0, tiled=True, axis_index_groups=CHIPS).reshape(16, block, C)

    back_of = [
        j * rows + d * local + r for d in range(n_dap) for r in range(local) for j in range(cols)
    ]
    d_pair = call(last_kernel, jax.ShapeDtypeStruct((block, C), BF16))(
        dn, loc, both, ln_attend[None], jnp.asarray(one_hot(back_of), BF16)
    )
    d_pair = lax.all_to_all(d_pair, "dap", 0, 0, tiled=True).reshape(n_dap, local, cols, C)
    pair_grad = d_pair.transpose(1, 0, 2, 3).reshape(local, n_cols, C).astype(F32)
    return (pair_grad, bias_grad)


def solution(mesh):
    in_specs = (
        P(("ctx", "dap"), None, None),
        P(("ctx", "dap"), None, None),
        P(),
        P(None, "ctx", None),
        P(),
        P(),
        P(),
        P(),
        P(),
        P(),
    )
    out_specs = (P(("ctx", "dap"), None, None), P(None, "ctx", "dap"))
    return jax.shard_map(
        per_device, mesh=mesh, in_specs=in_specs, out_specs=out_specs, check_vma=False
    )
```

```python
import numpy as np

import jax
import jax.numpy as jnp
from jax import lax
from jax.experimental import pallas as pl
from jax.experimental.pallas import tpu as pltpu
from jax.sharding import PartitionSpec as P

C = 128
H = 4
DH = 32
SCALE = DH ** (-0.5)
F32 = jnp.float32
BF16 = jnp.bfloat16
STEP = 16
UNROLL = 3

CORES = [[2 * m, 2 * m + 1] for m in range(16)]
CHIPS = [[2 * m + r for m in range(16)] for r in range(2)]


def mm(a, b):
    return jnp.dot(a, b, preferred_element_type=F32)


def mm_t(a, b):
    return lax.dot_general(a, b, (((1,), (1,)), ((), ())), preferred_element_type=F32)


def halves(x):
    hi = x.astype(BF16)
    return hi, (x - hi.astype(F32)).astype(BF16)


def center(x):
    mean = jnp.mean(x, axis=-1, keepdims=True)
    cen = x - mean
    var = jnp.mean(cen * cen, axis=-1, keepdims=True)
    rstd = lax.rsqrt(var + 1e-05)
    return cen * rstd, rstd


def center_back(hat, rstd, gain, d_out):
    t = d_out * gain
    a = jnp.mean(t, axis=-1, keepdims=True)
    b = jnp.mean(t * hat, axis=-1, keepdims=True)
    return rstd * (t - a - hat * b)


def prep_kernel(x_ref, order_ref, gain_ref, normed_ref, both_ref):
    both = mm(order_ref[...], x_ref[...])
    both_ref[...] = both
    hat, _ = center(both[: both.shape[0] // 2])
    normed_ref[...] = (hat * gain_ref[...]).astype(BF16)


def main_kernel(
    mine_ref, other_ref, normed_ref, both_ref, bias_ref, mask_ref, w_in_ref, w_out_ref, gain_ref, w_up_ref,
    w_down_ref,
    db_ref, keep_ref, send_ref, loc_ref,
    k_scr, v_scr, s_scr, e_scr, sum_scr, ds_scr, dsb_scr, dn_scr,
):
    n = bias_ref.shape[1]
    rows = bias_ref.shape[0] // H
    cols = 2
    block = cols * rows
    pairs = n // (2 * rows)
    core = lax.rem(lax.axis_index("ctx"), 2)
    first = core == 0

    batch = 4

    def make_kv(q, _):
        at = pl.ds(pl.multiple_of(q * batch * block, batch * block), batch * block)
        mine, other = mine_ref[at, :], other_ref[at, :]
        w_kv = w_in_ref[:, C : 3 * C]
        parts = [mm(jnp.where(first, mine, other), w_kv), mm(jnp.where(first, other, mine), w_kv)]
        for t in range(batch):
            dest = pl.ds(pl.multiple_of((q * batch + t) * 2 * rows, 2 * rows), 2 * rows)
            for j in range(cols):
                base = t * block + j * rows
                kv = jnp.concatenate([part[base : base + rows] for part in parts], axis=0).astype(BF16)
                k_scr[j, dest, :] = kv[:, :C]
                v_scr[j, dest, :] = kv[:, C:]
        return 0

    lax.fori_loop(0, pairs // batch, make_kv, 0)

    normed = normed_ref[...]
    queries = mm(normed, w_in_ref[:, :C])
    gate_raw = mm(normed, w_in_ref[:, 3 * C :])
    key_bias = (mask_ref[...].astype(F32) - 1.0) * 1000000000.0

    def head_mask(h):
        lane = lax.broadcasted_iota(jnp.int32, (rows, C), 1)
        return (lane >= h * DH) & (lane < (h + 1) * DH)

    def stack(x):
        return jnp.concatenate([jnp.where(head_mask(h), x, 0.0) for h in range(H)], axis=0)

    def unstack(x):
        out = jnp.where(head_mask(0), x[:rows], 0.0)
        for h in range(1, H):
            out = jnp.where(head_mask(h), x[h * rows : (h + 1) * rows], out)
        return out

    q_stack = [stack(queries[j * rows : (j + 1) * rows]) for j in range(cols)]
    heads = []
    for j in range(cols):
        s_scr[j] = mm_t(q_stack[j].astype(BF16), k_scr[j])

        def soft(r, _, j=j):
            at = pl.ds(pl.multiple_of(r * STEP, STEP), STEP)
            s = s_scr[j, at, :] * SCALE + bias_ref[at, :] + key_bias
            e = jnp.exp(s - jnp.max(s, axis=-1, keepdims=True))
            e_scr[j, at, :] = e.astype(BF16)
            sum_scr[j, at, :] = jnp.broadcast_to(jnp.sum(e, axis=-1, keepdims=True), (STEP, C))
            return 0

        lax.fori_loop(0, H * rows // STEP, soft, 0, unroll=UNROLL)
    inv = [1.0 / sum_scr[j] for j in range(cols)]
    o_stack = [mm(e_scr[j], v_scr[j]) * inv[j] for j in range(cols)]
    heads_out = jnp.concatenate([unstack(o) for o in o_stack], axis=0)

    open_ = jax.nn.sigmoid(gate_raw)
    source, cot = both_ref[:block, :], both_ref[block:, :]
    gated = (heads_out * open_).astype(BF16)
    mid = source + mm(gated, w_out_ref[...])
    mid_hat, mid_rstd = center(mid)
    gain = gain_ref[...]
    pre = mm((mid_hat * gain).astype(BF16), w_up_ref[...])
    gs = jax.nn.sigmoid(pre)
    slope = gs + pre * gs * (1.0 - gs)
    d_hidden = (mm_t(cot.astype(BF16), w_down_ref[...]) * slope).astype(BF16)
    d_trans = mm_t(d_hidden, w_up_ref[...])
    d_mid = cot + center_back(mid_hat, mid_rstd, gain, d_trans)
    d_gated = mm_t(d_mid.astype(BF16), w_out_ref[...])
    d_heads = d_gated * open_
    d_gate = d_gated * heads_out * open_ * (1.0 - open_)
    loc_ref[:block, :] = d_mid

    w_kv = w_in_ref[:, C : 3 * C]
    d_query = []
    for j in range(cols):
        do_f = stack(d_heads[j * rows : (j + 1) * rows]).astype(BF16).astype(F32) * inv[j]
        do_stack = do_f.astype(BF16)
        dot_row = jnp.sum(o_stack[j] * do_stack.astype(F32), axis=-1, keepdims=True)
        sum_scr[j] = jnp.broadcast_to(dot_row, (H * rows, C))
        s_scr[j] = mm_t(do_stack, v_scr[j])

        def back(r, _, j=j):
            at = pl.ds(pl.multiple_of(r * STEP, STEP), STEP)
            ds = e_scr[j, at, :].astype(F32) * (s_scr[j, at, :] - sum_scr[j, at, :1])
            dsb_scr[j, at, :] = ds.astype(BF16)
            if j == 0:
                ds_scr[at, :] = ds
            else:
                ds_scr[at, :] = ds_scr[at, :] + ds
            return 0

        lax.fori_loop(0, H * rows // STEP, back, 0, unroll=UNROLL)
        ds_b = dsb_scr[j]
        d_query.append(unstack(mm(ds_b, k_scr[j])) * SCALE)
        dk = mm(q_stack[j].T.astype(BF16), ds_b) * SCALE
        dv = mm(do_f.T.astype(BF16), e_scr[j])
        dn_scr[j] = mm(w_kv, jnp.concatenate([dk, dv], axis=0).astype(BF16)).T

    hi, lo = halves(jnp.concatenate([jnp.concatenate(d_query, axis=0), d_gate], axis=1))
    w_qg = jnp.concatenate([w_in_ref[:, :C], w_in_ref[:, 3 * C :]], axis=1)
    loc_ref[block:, :] = mm_t(hi, w_qg) + mm_t(lo, w_qg)

    for p in range(pairs):
        place = sum(((p >> bit) & 1) << to for bit, to in ((0, 0), (3, 1), (2, 2), (1, 3))) * block
        for ref, which in ((keep_ref, core), (send_ref, 1 - core)):
            at = pl.ds(pl.multiple_of((2 * p + which) * rows, rows), rows)
            both = jnp.concatenate([dn_scr[j, at, :] for j in range(cols)], axis=0)
            ref[place : place + block, :] = both.astype(ref.dtype)

    def put_db(t, _):
        at = pl.ds(pl.multiple_of(t * C, C), C)
        xs = [ds_scr[pl.ds(h * rows, rows), at] for h in range(H)]
        groups = []
        for a in range(4):
            out = xs[a]
            for h in range(H):
                if h != a:
                    out = jnp.where(head_mask(h), pltpu.roll(xs[h], ((h - a) * DH) % C, 1), out)
            groups.append(out)
        start = pl.multiple_of(t * 4 * rows, 4 * rows)
        db_ref[pl.ds(start, 4 * rows), :] = jnp.concatenate(groups, axis=0).astype(BF16)
        return 0

    lax.fori_loop(0, n // C, put_db, 0)


def last_kernel(parts_ref, loc_ref, both_ref, gain_ref, order_ref, after_ref, out_ref):
    del after_ref
    half = loc_ref.shape[0] // 2
    total = loc_ref[half:, :] + parts_ref[...]
    hat, rstd = center(both_ref[:half, :])
    d_pair = loc_ref[:half, :] + center_back(hat, rstd, gain_ref[...], total)
    out_ref[...] = mm(order_ref[...], d_pair.astype(BF16)).astype(BF16)


def bias_kernel(parts_ref, out_ref):
    rows = out_ref.shape[1]
    total = parts_ref[0].astype(F32)
    for p in range(1, parts_ref.shape[0]):
        total = total + parts_ref[p].astype(F32)
    for h in range(H):
        out_ref[h] = jnp.concatenate(
            [total[t * rows : (t + 1) * rows, h * DH : (h + 1) * DH] for t in range(3)], axis=1
        )


def call(kernel, out_shape, scratch=(), limit=48, n_in=None, unread=0):
    specs = {}
    if unread:
        vmem = pl.BlockSpec(memory_space=pltpu.VMEM)
        specs["in_specs"] = [vmem] * (n_in - unread) + [pl.BlockSpec(memory_space=pl.ANY)] * unread
    return pl.pallas_call(
        kernel,
        out_shape=out_shape,
        **specs,
        scratch_shapes=list(scratch),
        compiler_params=pltpu.CompilerParams(vmem_limit_bytes=limit * 1024 * 1024),
    )


def one_hot(source_of):
    out = np.zeros((len(source_of), len(source_of)), np.float32)
    out[np.arange(len(source_of)), source_of] = 1.0
    return out


def per_device(pair, cotangent, residue_mask, bias, ln_attend, w_in, w_out, ln_trans, w_up, w_down):
    n_dap = lax.axis_size("dap")
    n_ctx = lax.axis_size("ctx")
    local, n_cols, _ = pair.shape
    cols = n_cols // n_dap
    rows = local * n_dap
    n = rows * n_ctx
    block = cols * rows
    each = cols * local

    both = jnp.stack([pair, cotangent]).reshape(2, local, n_dap, cols, C)
    both = both.transpose(2, 0, 3, 1, 4).reshape(n_dap * 2 * each, C)
    both = lax.all_to_all(both, "dap", 0, 0, tiled=True)
    source_of = [
        (i // local) * 2 * each + a * each + j * local + i % local
        for a in range(2)
        for j in range(cols)
        for i in range(rows)
    ]
    normed, both = call(
        prep_kernel,
        (jax.ShapeDtypeStruct((block, C), BF16), jax.ShapeDtypeStruct((2 * block, C), F32)),
    )(both, jnp.asarray(one_hot(source_of), BF16), ln_attend[None])

    gathered = jnp.broadcast_to(normed[None], (n_ctx // 2, block, C)).reshape(n_ctx // 2 * block, C)
    gathered = lax.all_to_all(gathered, "ctx", 0, 0, tiled=True, axis_index_groups=CHIPS)
    other = lax.ppermute(gathered, "ctx", [(i, i ^ 1) for i in range(n_ctx)])

    half = jax.ShapeDtypeStruct((n * cols // 2, C), F32)
    db, keep, send, loc = call(
        main_kernel,
        (
            jax.ShapeDtypeStruct((n // DH * rows, C), BF16),
            half,
            jax.ShapeDtypeStruct(half.shape, BF16),
            jax.ShapeDtypeStruct((2 * block, C), F32),
        ),
        scratch=(
            pltpu.VMEM((cols, n, C), BF16),
            pltpu.VMEM((cols, n, C), BF16),
            pltpu.VMEM((cols, H * rows, n), F32),
            pltpu.VMEM((cols, H * rows, n), BF16),
            pltpu.VMEM((cols, H * rows, C), F32),
            pltpu.VMEM((H * rows, n), F32),
            pltpu.VMEM((cols, H * rows, n), BF16),
            pltpu.VMEM((cols, n, C), F32),
        ),
        limit=40,
    )(
        gathered, other, normed, both, bias.reshape(H * rows, n), residue_mask[None], w_in, w_out, ln_trans[None],
        w_up, w_down,
    )

    db = lax.all_to_all(db, "dap", 0, 0, tiled=True).reshape(n_dap, n // n_dap // DH * rows, C)

    here = lax.axis_index("ctx")
    total = keep + lax.ppermute(send, "ctx", [(i, i ^ 1) for i in range(n_ctx)]).astype(F32)
    for flip in (4, 8, 16, 2):
        total = total.reshape(2, -1, C)
        bit = jnp.where((here & flip) != 0, 1, 0)
        kept = lax.dynamic_index_in_dim(total, bit, 0, False)
        sent = lax.dynamic_index_in_dim(total, 1 - bit, 0, False).astype(BF16)
        total = kept + lax.ppermute(sent, "ctx", [(i, i ^ flip) for i in range(n_ctx)]).astype(F32)

    back_of = [
        j * rows + d * local + r for d in range(n_dap) for r in range(local) for j in range(cols)
    ]
    d_pair = call(last_kernel, jax.ShapeDtypeStruct((block, C), BF16), n_in=6, unread=1)(
        total, loc, both, ln_attend[None], jnp.asarray(one_hot(back_of), BF16), db
    )
    bias_grad = call(bias_kernel, jax.ShapeDtypeStruct((H, rows, n // n_dap), F32))(db)
    d_pair = lax.all_to_all(d_pair, "dap", 0, 0, tiled=True).reshape(n_dap, local, cols, C)
    pair_grad = d_pair.transpose(1, 0, 2, 3).reshape(local, n_cols, C).astype(F32)
    return (pair_grad, bias_grad)


def solution(mesh):
    in_specs = (
        P(("ctx", "dap"), None, None),
        P(("ctx", "dap"), None, None),
        P(),
        P(None, "ctx", None),
        P(),
        P(),
        P(),
        P(),
        P(),
        P(),
    )
    out_specs = (P(("ctx", "dap"), None, None), P(None, "ctx", "dap"))
    return jax.shard_map(
        per_device, mesh=mesh, in_specs=in_specs, out_specs=out_specs, check_vma=False
    )
```

```python
import jax
import jax.numpy as jnp
from jax import lax
from jax.experimental import pallas as pl
from jax.experimental.pallas import tpu as pltpu
from jax.sharding import PartitionSpec as P

C = 128
H = 4
DH = 32
SCALE = DH ** (-0.5)
F32 = jnp.float32
BF16 = jnp.bfloat16
STEP = 16
UNROLL = 18
UDB = 6
LIMIT = 40
FLIPS = ((4, 8, 12), (2, 16, 18))

CORES = [[2 * m, 2 * m + 1] for m in range(16)]
CHIPS = [[2 * m + r for m in range(16)] for r in range(2)]


def mm(a, b):
    return jnp.dot(a, b, preferred_element_type=F32)


def mm_t(a, b):
    return lax.dot_general(a, b, (((1,), (1,)), ((), ())), preferred_element_type=F32)


def halves(x):
    hi = x.astype(BF16)
    return hi, (x - hi.astype(F32)).astype(BF16)


def center(x):
    mean = jnp.mean(x, axis=-1, keepdims=True)
    cen = x - mean
    var = jnp.mean(cen * cen, axis=-1, keepdims=True)
    rstd = lax.rsqrt(var + 1e-05)
    return cen * rstd, rstd


def center_back(hat, rstd, gain, d_out):
    t = d_out * gain
    a = jnp.mean(t, axis=-1, keepdims=True)
    b = jnp.mean(t * hat, axis=-1, keepdims=True)
    return rstd * (t - a - hat * b)


def iotas(rows, cols):
    shape = (rows, cols)
    return lax.broadcasted_iota(jnp.int32, shape, 0), lax.broadcasted_iota(jnp.int32, shape, 1)


def split8(at, local):
    q = at & 7
    j = jnp.where(q >= local, 1, 0)
    return j, q - local * j, q < 2 * local


def pick(where):
    return jnp.where(where, 1.0, 0.0).astype(BF16)


def first_kernel(pair_ref, cot_ref, out_ref):
    local, n_cols, _ = pair_ref.shape
    each = local * n_cols
    tokens = jnp.concatenate([pair_ref[...].reshape(each, C), cot_ref[...].reshape(each, C)], axis=0)
    out, at = iotas(out_ref.shape[0], 2 * each)
    j, r, valid = split8(out, local)
    source = ((out >> 3) & 1) * each + r * n_cols + (out >> 4) * 2 + j
    out_ref[...] = mm(pick(valid & (at == source)), tokens).astype(BF16)


def prep_kernel(x_ref, gain_ref, normed_ref, both_ref):
    block = normed_ref.shape[0]
    local = block // 2 // (x_ref.shape[0] // 16)
    out, at = iotas(2 * block, x_ref.shape[0])
    j, r, valid = split8(at, local)
    goal = ((at >> 3) & 1) * block + j * (block // 2) + (at >> 4) * local + r
    both = mm(pick(valid & (out == goal)), x_ref[...])
    both_ref[...] = both
    hat, _ = center(both[:block])
    normed_ref[...] = (hat * gain_ref[...]).astype(BF16)


def relative(place):
    return (place >> 2 << 1) | ((place >> 1 & 1) << 3) | (place & 1)


def main_kernel(
    mine_ref, other_ref, normed_ref, both_ref, bias_ref, mask_ref, w_in_ref, w_out_ref, gain_ref, w_up_ref,
    w_down_ref,
    db_out, keep_out, send_out, loc_out,
    db_ref, keep_ref, send_ref, loc_ref, sems,
    k_scr, v_scr, s_scr, e_scr, sum_scr, ds_scr, dsb_scr, dn_scr,
):
    n = bias_ref.shape[1]
    rows = bias_ref.shape[0] // H
    cols = 2
    block = cols * rows
    pairs = n // (2 * rows)
    core = lax.rem(lax.axis_index("ctx"), 2)
    first = core == 0

    outs = ((db_ref, db_out), (keep_ref, keep_out), (send_ref, send_out), (loc_ref, loc_out))
    copies = [pltpu.make_async_copy(src, dst, sems.at[i]) for i, (src, dst) in enumerate(outs)]
    batch = 4

    def make_kv(q, _):
        at = pl.ds(pl.multiple_of(q * batch * block, batch * block), batch * block)
        mine, other = mine_ref[at, :], other_ref[at, :]
        w_kv = w_in_ref[:, C : 3 * C]
        parts = [mm(jnp.where(first, mine, other), w_kv), mm(jnp.where(first, other, mine), w_kv)]
        for t in range(batch):
            dest = pl.ds(pl.multiple_of((q * batch + t) * 2 * rows, 2 * rows), 2 * rows)
            for j in range(cols):
                base = t * block + j * rows
                kv = jnp.concatenate([part[base : base + rows] for part in parts], axis=0).astype(BF16)
                k_scr[j, dest, :] = kv[:, :C]
                v_scr[j, dest, :] = kv[:, C:]
        return 0

    lax.fori_loop(0, pairs // batch, make_kv, 0)

    normed = normed_ref[...]
    queries = mm(normed, w_in_ref[:, :C])
    gate_raw = mm(normed, w_in_ref[:, 3 * C :])
    key_bias = (mask_ref[...].astype(F32) - 1.0) * 1000000000.0

    def head_mask(h):
        lane = lax.broadcasted_iota(jnp.int32, (rows, C), 1)
        return (lane >= h * DH) & (lane < (h + 1) * DH)

    def stack(x):
        return jnp.concatenate([jnp.where(head_mask(h), x, 0.0) for h in range(H)], axis=0)

    def unstack(x):
        out = jnp.where(head_mask(0), x[:rows], 0.0)
        for h in range(1, H):
            out = jnp.where(head_mask(h), x[h * rows : (h + 1) * rows], out)
        return out

    q_stack = [stack(queries[j * rows : (j + 1) * rows]) for j in range(cols)]
    for j in range(cols):
        s_scr[j] = mm_t(q_stack[j].astype(BF16), k_scr[j])

    def soft(r, _):
        at = pl.ds(pl.multiple_of(r * STEP, STEP), STEP)
        bias = bias_ref[at, :]
        for j in range(cols):
            s = s_scr[j, at, :] * SCALE + bias + key_bias
            e = jnp.exp(s - jnp.max(s, axis=-1, keepdims=True))
            e_scr[j, at, :] = e.astype(BF16)
            sum_scr[j, at, :] = jnp.broadcast_to(jnp.sum(e, axis=-1, keepdims=True), (STEP, C))
        return 0

    lax.fori_loop(0, H * rows // STEP, soft, 0, unroll=UNROLL)
    inv = [1.0 / sum_scr[j] for j in range(cols)]
    o_stack = [mm(e_scr[j], v_scr[j]) * inv[j] for j in range(cols)]
    heads_out = jnp.concatenate([unstack(o) for o in o_stack], axis=0)

    open_ = jax.nn.sigmoid(gate_raw)
    source, cot = both_ref[:block, :], both_ref[block:, :]
    gated = (heads_out * open_).astype(BF16)
    mid = source + mm(gated, w_out_ref[...])
    mid_hat, mid_rstd = center(mid)
    gain = gain_ref[...]
    pre = mm((mid_hat * gain).astype(BF16), w_up_ref[...])
    gs = jax.nn.sigmoid(pre)
    slope = gs + pre * gs * (1.0 - gs)
    d_hidden = (mm_t(cot.astype(BF16), w_down_ref[...]) * slope).astype(BF16)
    d_trans = mm_t(d_hidden, w_up_ref[...])
    d_mid = cot + center_back(mid_hat, mid_rstd, gain, d_trans)
    d_gated = mm_t(d_mid.astype(BF16), w_out_ref[...])
    d_heads = d_gated * open_
    d_gate = d_gated * heads_out * open_ * (1.0 - open_)
    loc_ref[:block, :] = d_mid

    w_kv = w_in_ref[:, C : 3 * C]
    d_query, do_t = [], []
    for j in range(cols):
        do_f = stack(d_heads[j * rows : (j + 1) * rows]).astype(BF16).astype(F32) * inv[j]
        do_stack = do_f.astype(BF16)
        do_t.append(do_f.T.astype(BF16))
        dot_row = jnp.sum(o_stack[j] * do_stack.astype(F32), axis=-1, keepdims=True)
        sum_scr[j] = jnp.broadcast_to(dot_row, (H * rows, C))
        s_scr[j] = mm_t(do_stack, v_scr[j])

    def back(r, _):
        at = pl.ds(pl.multiple_of(r * STEP, STEP), STEP)
        total = None
        for j in range(cols):
            ds = e_scr[j, at, :].astype(F32) * (s_scr[j, at, :] - sum_scr[j, at, :1])
            dsb_scr[j, at, :] = ds.astype(BF16)
            total = ds if total is None else total + ds
        ds_scr[at, :] = total
        return 0

    lax.fori_loop(0, H * rows // STEP, back, 0, unroll=UNROLL)
    lane = lax.broadcasted_iota(jnp.int32, (rows, C), 1)

    def put_db(t, _):
        at = pl.ds(pl.multiple_of(t * C, C), C)
        xs = [ds_scr[pl.ds(h * rows, rows), at] for h in range(H)]
        low, even = (lane & 64) == 0, (lane & 32) == 0
        ys = [None] * H
        for h in range(2):
            ys[h] = jnp.where(low, xs[h], pltpu.roll(xs[h + 2], 64, 1))
            ys[h + 2] = jnp.where(low, pltpu.roll(xs[h], 64, 1), xs[h + 2])
        groups = []
        for h in (0, 2):
            groups.append(jnp.where(even, ys[h], pltpu.roll(ys[h + 1], 32, 1)))
            groups.append(jnp.where(even, pltpu.roll(ys[h], 96, 1), ys[h + 1]))
        start = pl.multiple_of(t * 4 * rows, 4 * rows)
        db_ref[pl.ds(start, 4 * rows), :] = jnp.concatenate(groups, axis=0).astype(BF16)
        return 0

    lax.fori_loop(0, n // C, put_db, 0, unroll=UDB)
    copies[0].start()

    for j in range(cols):
        ds_b = dsb_scr[j]
        d_query.append(unstack(mm(ds_b, k_scr[j])) * SCALE)
        dk = mm(q_stack[j].T.astype(BF16), ds_b) * SCALE
        dv = mm(do_t[j], e_scr[j])
        dn_scr[j] = mm(w_kv, jnp.concatenate([dk, dv], axis=0).astype(BF16)).T

    hi, lo = halves(jnp.concatenate([jnp.concatenate(d_query, axis=0), d_gate], axis=1))
    w_qg = jnp.concatenate([w_in_ref[:, :C], w_in_ref[:, 3 * C :]], axis=1)
    loc_ref[block:, :] = mm_t(hi, w_qg) + mm_t(lo, w_qg)
    copies[3].start()

    chip = lax.div(lax.axis_index("ctx"), 2)
    for place in range(pairs):
        p = lax.bitwise_xor(chip, relative(place))
        for ref, which in ((keep_ref, core), (send_ref, 1 - core)):
            at = pl.ds(pl.multiple_of((2 * p + which) * rows, rows), rows)
            both = jnp.concatenate([dn_scr[j, at, :] for j in range(cols)], axis=0)
            ref[place * block : (place + 1) * block, :] = both.astype(ref.dtype)

    copies[1].start()
    copies[2].start()
    for copy in copies:
        copy.wait()


def quarter_kernel(keep_ref, *refs):
    parts, (kept_ref, *sent) = refs[: -4], refs[-4 :]
    size = kept_ref.shape[0]
    for q in range(4):
        at = slice(q * size, (q + 1) * size)
        total = keep_ref[at, :]
        for part in parts:
            total = total + part[at, :].astype(F32)
        if q == 0:
            kept_ref[...] = total
        else:
            sent[q - 1][...] = total.astype(BF16)


def last_kernel(kept_ref, a_ref, b_ref, c_ref, loc_ref, both_ref, gain_ref, after_ref, out_ref):
    del after_ref
    half = loc_ref.shape[0] // 2
    total = loc_ref[half:, :] + kept_ref[...]
    for part in (a_ref, b_ref, c_ref):
        total = total + part[...].astype(F32)
    hat, rstd = center(both_ref[:half, :])
    d_pair = loc_ref[:half, :] + center_back(hat, rstd, gain_ref[...], total)
    local = half // 2 // (out_ref.shape[0] // 8)
    out, at = iotas(out_ref.shape[0], half)
    j, r, valid = split8(out, local)
    order = pick(valid & (at == j * (half // 2) + (out >> 3) * local + r))
    out_ref[...] = mm(order, d_pair.astype(BF16)).astype(BF16)


def finish_kernel(x_ref, out_ref):
    local, n_cols, _ = out_ref.shape
    out, at = iotas(local * n_cols, x_ref.shape[0])
    j, r, valid = split8(at, local)
    order = pick(valid & (out == r * n_cols + (at >> 3) * 2 + j))
    out_ref[...] = mm(order, x_ref[...]).reshape(out_ref.shape)


def bias_kernel(parts_ref, out_ref):
    rows = out_ref.shape[1]
    total = parts_ref[0].astype(F32)
    for p in range(1, parts_ref.shape[0]):
        total = total + parts_ref[p].astype(F32)
    for h in range(H):
        out_ref[h] = jnp.concatenate(
            [total[t * rows : (t + 1) * rows, h * DH : (h + 1) * DH] for t in range(3)], axis=1
        )


def call(kernel, out_shape, limit=16, n_in=None, unread=0):
    specs = {}
    if unread:
        vmem = pl.BlockSpec(memory_space=pltpu.VMEM)
        specs["in_specs"] = [vmem] * (n_in - unread) + [pl.BlockSpec(memory_space=pl.ANY)] * unread
    return pl.pallas_call(
        kernel,
        out_shape=out_shape,
        **specs,
        compiler_params=pltpu.CompilerParams(vmem_limit_bytes=limit * 1024 * 1024),
    )


def run_main(mine, other, normed, both, bias, mask, *weights):
    cols, n = 2, bias.shape[1]
    rows = bias.shape[0] // H
    block = cols * rows
    outs = (
        ((n // DH * rows, C), BF16),
        ((n * cols // 2, C), F32),
        ((n * cols // 2, C), BF16),
        ((2 * block, C), F32),
    )
    scratch = [pltpu.VMEM(shape, dtype) for shape, dtype in outs]
    scratch += [pltpu.SemaphoreType.DMA((len(outs),))]
    scratch += [
        pltpu.VMEM((cols, n, C), BF16),
        pltpu.VMEM((cols, n, C), BF16),
        pltpu.VMEM((cols, H * rows, n), F32),
        pltpu.VMEM((cols, H * rows, n), BF16),
        pltpu.VMEM((cols, H * rows, C), F32),
        pltpu.VMEM((H * rows, n), F32),
        pltpu.VMEM((cols, H * rows, n), BF16),
        pltpu.VMEM((cols, n, C), F32),
    ]
    return pl.pallas_call(
        main_kernel,
        out_shape=[jax.ShapeDtypeStruct(shape, dtype) for shape, dtype in outs],
        out_specs=[pl.BlockSpec(memory_space=pltpu.HBM)] * len(outs),
        scratch_shapes=scratch,
        compiler_params=pltpu.CompilerParams(vmem_limit_bytes=LIMIT * 1024 * 1024),
    )(mine, other, normed, both, bias, mask, *weights)


def per_device(pair, cotangent, residue_mask, bias, ln_attend, w_in, w_out, ln_trans, w_up, w_down):
    n_dap = lax.axis_size("dap")
    n_ctx = lax.axis_size("ctx")
    local, n_cols, _ = pair.shape
    cols = n_cols // n_dap
    rows = local * n_dap
    n = rows * n_ctx
    block = cols * rows

    x = call(first_kernel, jax.ShapeDtypeStruct((n_dap * 16, C), BF16))(pair, cotangent)
    x = lax.all_to_all(x, "dap", 0, 0, tiled=True)
    normed, both = call(
        prep_kernel,
        (jax.ShapeDtypeStruct((block, C), BF16), jax.ShapeDtypeStruct((2 * block, C), F32)),
    )(x, ln_attend[None])

    gathered = jnp.broadcast_to(normed[None], (n_ctx // 2, block, C)).reshape(n_ctx // 2 * block, C)
    gathered = lax.all_to_all(gathered, "ctx", 0, 0, tiled=True, axis_index_groups=CHIPS)
    other = lax.ppermute(gathered, "ctx", [(i, i ^ 1) for i in range(n_ctx)])

    db, keep, send, loc = run_main(
        gathered, other, normed, both, bias.reshape(H * rows, n), residue_mask[None], w_in, w_out, ln_trans[None],
        w_up, w_down,
    )
    db = lax.all_to_all(db, "dap", 0, 0, tiled=True).reshape(n_dap, n // n_dap // DH * rows, C)

    parts = [lax.ppermute(send, "ctx", [(i, i ^ 1) for i in range(n_ctx)])]
    for flips in FLIPS:
        size = keep.shape[0] // 4
        shapes = [jax.ShapeDtypeStruct((size, C), dtype) for dtype in (F32, BF16, BF16, BF16)]
        keep, *sent = call(quarter_kernel, shapes)(keep, *parts)
        parts = [lax.ppermute(part, "ctx", [(i, i ^ flip) for i in range(n_ctx)]) for part, flip in zip(sent, flips)]

    d_pair = call(last_kernel, jax.ShapeDtypeStruct((n_dap * 8, C), BF16), n_in=8, unread=1)(
        keep, *parts, loc, both, ln_attend[None], db
    )
    bias_grad = call(bias_kernel, jax.ShapeDtypeStruct((H, rows, n // n_dap), F32))(db)
    d_pair = lax.all_to_all(d_pair, "dap", 0, 0, tiled=True)
    pair_grad = call(finish_kernel, jax.ShapeDtypeStruct((local, n_cols, C), F32))(d_pair)
    return (pair_grad, bias_grad)


def solution(mesh):
    in_specs = (
        P(("ctx", "dap"), None, None),
        P(("ctx", "dap"), None, None),
        P(),
        P(None, "ctx", None),
        P(),
        P(),
        P(),
        P(),
        P(),
        P(),
    )
    out_specs = (P(("ctx", "dap"), None, None), P(None, "ctx", "dap"))
    return jax.shard_map(
        per_device, mesh=mesh, in_specs=in_specs, out_specs=out_specs, check_vma=False
    )
```
